32 devices in a mesh: wide: 8 (over z, y), narrow: 4 (over x, core).
Axes of the slice: x: 2, y: 2, z: 4, core: 2. Of those that a mesh axis runs over, the one named last changes fastest.
Arguments:
- resid: bfloat16 [128, 16384], P(('wide', 'narrow')), may hold values from -6 to 6
- queries: bfloat16 [128, 16384], P(('wide', 'narrow')), may hold values from -9 to 9
- key_cache: bfloat16 [128, 192, 1024], P(('wide', 'narrow')), may hold values from -4 to 4
- value_cache: bfloat16 [128, 192, 1024], P(('wide', 'narrow')), may hold values from -6 to 6
- new_keys: bfloat16 [128, 1024], P(('wide', 'narrow')), may hold values from -4 to 4
- new_values: bfloat16 [128, 1024], P(('wide', 'narrow')), may hold values from -6 to 6
- lengths: int32 [128], P(('wide', 'narrow')), may hold values from 2 to 192, as said below
- norm_gain: bfloat16 [16384], replicated, may hold values from 0.099609375 to 1.8984375
- w_gate: bfloat16 [16384, 28672], P('narrow', 'wide'), may hold values from -0.046875 to 0.046875
- w_up: bfloat16 [16384, 28672], P('narrow', 'wide'), may hold values from -0.046875 to 0.046875
- w_down: bfloat16 [28672, 16384], P('wide', 'narrow'), may hold values from -0.03125 to 0.03125
Outputs:
- layer_out: bfloat16 [128, 16384], P(('wide', 'narrow'))
The draws below stay inside these ranges and needn't reach their ends.
Inputs may be any that keep to these rules, and one draw needn't show every extreme that they name: Positions below lengths[b] of sequence b are live; some sequence holds all 192.
All inputs are finite; a program needn't handle non-finite values.
Results may differ from the reference program's by a relative error of at most 0.019.
Values may be sent and summed in bfloat16 or wider, within the bound.
No kernel may reach another device: no remote copies, remote signals or barrier semaphores. Data moves between devices by JAX's collectives and lax.ppermute only.
A program may use at most 192 MiB of HBM per device.

```python
import jax
import jax.numpy as jnp
from jax import lax

CACHE = 192
D = 16384
FF = 28672
HEADS = 128
KVH = 8
HD = 128
BATCH = 128
N_WIDE = 8
N_NARROW = 4


def draw_queries(key, part):
    columns = HEADS * HD
    values = jnp.clip(jax.random.normal(key, (BATCH, columns), jnp.float32), -6.0, 6.0)
    return values.astype(jnp.bfloat16)


def draw_key_cache(key, part):
    columns = KVH * HD
    values = jnp.clip(jax.random.normal(key, (BATCH, CACHE, columns), jnp.float32), -4.0, 4.0)
    return values.astype(jnp.bfloat16)


def draw_lengths(key, part):
    drawn = jax.random.randint(key, (BATCH,), 2, CACHE + 1, dtype=jnp.int32)
    where_full = jax.random.randint(jax.random.fold_in(key, 11), (), 0, BATCH, dtype=jnp.int32)
    return drawn.at[where_full].set(CACHE)


def shard_levels(own_key, shape, split, least, largest):
    level = 1.0
    for axis_at, blocks in split:
        heights = jax.random.uniform(jax.random.fold_in(jax.random.fold_in(own_key, 6), axis_at), (blocks,), jnp.float32, least / len(split), largest / len(split))
        level = level * jnp.repeat(jnp.exp(heights), shape[axis_at] // blocks).reshape((-1,) + (1,) * (len(shape) - 1 - axis_at))
    return level


def gaussian(own_key, shape, scale, reach, cuts=(), held_as=jnp.bfloat16):
    loudness = shard_levels(own_key, shape, cuts, -0.22, 0.18) if cuts else 1.0
    array = jax.random.normal(own_key, shape, jnp.float32) * scale * loudness
    return jnp.minimum(jnp.maximum(array, -reach), reach).astype(held_as)


def setup_inputs(seed: int = 0) -> dict:
    splits = jax.random.split(jax.random.key(seed), 12)
    resid = gaussian(splits[0], (BATCH, D), 1.0, 6.0, ((0, 32),))
    queries = draw_queries(jax.random.fold_in(splits[11], 71), 0)
    key_cache = draw_key_cache(jax.random.fold_in(splits[11], 71), 0)
    value_cache = gaussian(splits[3], (BATCH, CACHE, KVH * HD), 1.0, 6.0, ((0, 32),))
    new_keys = gaussian(splits[4], (BATCH, KVH * HD), 1.0, 4.0, ((0, 32),))
    new_values = gaussian(splits[5], (BATCH, KVH * HD), 1.0, 6.0, ((0, 32),))
    lengths = draw_lengths(jax.random.fold_in(splits[11], 71), 0)
    norm_gain = jnp.clip(1.0 + 0.18 * jax.random.normal(splits[7], (D,), jnp.float32), 0.099609375, 1.8984375).astype(jnp.bfloat16)
    w_gate = gaussian(splits[8], (D, FF), D ** -0.5, 0.046875, ((0, 4), (1, 8)))
    w_up = gaussian(splits[9], (D, FF), D ** -0.5, 0.046875, ((0, 4), (1, 8)))
    w_down = gaussian(splits[10], (FF, D), FF ** -0.5, 0.03125, ((0, 8), (1, 4)))
    return {"resid": resid, "queries": queries, "key_cache": key_cache, "value_cache": value_cache, "new_keys": new_keys, "new_values": new_values, "lengths": lengths, "norm_gain": norm_gain, "w_gate": w_gate, "w_up": w_up, "w_down": w_down}


def attend(query_rows, key_rows, value_rows, key_new, value_new, length_rows):
    count = query_rows.shape[0]
    groups = HEADS // KVH
    qh = query_rows.reshape(count, KVH, groups, HD).astype(jnp.float32)
    kh = key_rows.reshape(count, CACHE, KVH, HD).astype(jnp.float32)
    vh = value_rows.reshape(count, CACHE, KVH, HD).astype(jnp.float32)
    kn = key_new.reshape(count, KVH, HD).astype(jnp.float32)
    vn = value_new.reshape(count, KVH, HD).astype(jnp.float32)
    score_scale = 1.0 / HD ** 0.5
    scores = jnp.einsum('bgqd,btgd->bgqt', qh, kh) * score_scale
    own = jnp.einsum('bgqd,bgd->bgq', qh, kn) * score_scale
    live = jnp.arange(CACHE, dtype=jnp.int32)[None, :] < length_rows[:, None]
    live = live[:, None, None, :]
    scores = jnp.where(live, scores, jnp.float32(-1e+30))
    row_top = jnp.maximum(lax.optimization_barrier(jnp.max(scores, axis=-1)), own)
    cache_exp = jnp.where(live, jnp.exp(scores - row_top[..., None]), jnp.float32(0.0))
    own_exp = jnp.exp(own - row_top)
    total = lax.optimization_barrier(jnp.sum(cache_exp, axis=-1)) + own_exp
    probs = (cache_exp / total[..., None]).astype(jnp.bfloat16)
    own_prob = (own_exp / total).astype(jnp.bfloat16)
    attended = jnp.einsum('bgqt,btgd->bgqd', probs.astype(jnp.float32), vh)
    attended = attended + own_prob.astype(jnp.float32)[..., None] * vn[:, :, None, :]
    return attended.reshape(count, HEADS * HD)

def blocked_product(left, right, blocks):
    width = left.shape[1] // blocks
    total = jnp.zeros((left.shape[0], right.shape[1]), jnp.float32)
    for block in range(blocks):
        term = jnp.dot(left[:, block * width:(block + 1) * width], right[block * width:(block + 1) * width], preferred_element_type=jnp.float32)
        total = total + term.astype(jnp.bfloat16).astype(jnp.float32)
    return total

def reference(resid, queries, key_cache, value_cache, new_keys, new_values, lengths, norm_gain, w_gate, w_up, w_down):

    def single(items):
        picked = [item[None] for item in items]
        return attend(*picked)[0]
    attended = lax.map(single, (queries, key_cache, value_cache, new_keys, new_values, lengths))
    mixed = resid.astype(jnp.float32) + attended
    mean_square = lax.optimization_barrier(jnp.mean(mixed * mixed, axis=-1, keepdims=True))
    normed = (mixed * lax.rsqrt(mean_square + 1e-05) * norm_gain.astype(jnp.float32)).astype(jnp.bfloat16)
    gate = blocked_product(normed, w_gate, N_NARROW)
    up_rows = blocked_product(normed, w_up, N_NARROW)
    hidden = (jax.nn.silu(gate) * up_rows).astype(jnp.bfloat16)
    ffn_out = blocked_product(hidden, w_down, N_WIDE).astype(jnp.bfloat16)
    return (mixed + ffn_out.astype(jnp.float32)).astype(jnp.bfloat16)
```

```python
import jax
import jax.numpy as jnp
from jax import lax
from jax.experimental import pallas as pl
from jax.experimental.pallas import tpu as pltpu
from jax.sharding import PartitionSpec as P

HEADS = 128
KVH = 8
HD = 128
F32 = jnp.float32
BF16 = jnp.bfloat16
COST = 16
SCOPED = 3 << 20
def tile_of(width):
    for tile in (512, 256, 128):
        if width % tile == 0:
            return tile
    return width


def after(x, *others):
    return lax.optimization_barrier((x, *others))[0]


SCALAR = pl.BlockSpec(memory_space=pltpu.SMEM)
FAST = pl.BlockSpec(memory_space=pltpu.VMEM)
SLOW = pl.BlockSpec(memory_space=pltpu.HBM)
ANY = pl.BlockSpec(memory_space=pl.ANY)


class Piece:
    def __init__(self, weight, row, rows, column, columns):
        self.weight = weight
        self.row, self.rows, self.column, self.columns = row, rows, column, columns


def call(kernel, name, flags, inputs, outputs, ahead, scratch, flops, behind):
    weights = []
    for piece in ahead:
        if not any(piece.weight is w for w in weights):
            weights.append(piece.weight)
    source = [next(i for i, w in enumerate(weights) if w is p.weight) for p in ahead]
    n_in, n_w, n_out, n_a = len(inputs), len(weights), len(outputs), len(ahead)

    def whole(*refs):
        flag_ref, refs = refs[0], refs[1:]
        in_refs, refs = refs[:n_in], refs[n_in + len(behind) :]
        weight_refs, refs = refs[:n_w], refs[n_w:]
        out_refs, refs = refs[:n_out], refs[n_out:]
        ahead_refs, refs = refs[:n_a], refs[n_a:]
        sems, scratch_refs = refs[0], refs[1:]
        copies = []
        for i, piece in enumerate(ahead):
            view = weight_refs[source[i]].at[
                pl.ds(piece.row, piece.rows), pl.ds(piece.column, piece.columns)
            ]
            copies.append(pltpu.make_async_copy(view, ahead_refs[i], sems.at[i]))
        for copy in copies:
            copy.start()
        kernel(flag_ref, in_refs, out_refs, scratch_refs)
        for copy in copies:
            copy.wait()

    moved = sum(2 * p.rows * p.columns for p in ahead)
    result = pl.pallas_call(
        whole,
        in_specs=[SCALAR, *[FAST] * n_in, *[ANY] * len(behind), *[SLOW] * n_w],
        out_specs=[FAST] * (n_out + n_a),
        out_shape=[*outputs, *[jax.ShapeDtypeStruct((p.rows, p.columns), BF16) for p in ahead]],
        scratch_shapes=[pltpu.SemaphoreType.DMA((max(1, n_a),)), *scratch],
        compiler_params=pltpu.CompilerParams(vmem_limit_bytes=SCOPED),
        cost_estimate=pl.CostEstimate(
            flops=flops // COST, bytes_accessed=moved // COST, transcendentals=0
        ),
        name=name,
    )(flags, *inputs, *behind, *[pltpu.with_memory_space_constraint(w, pltpu.HBM) for w in weights])
    return result[:n_out], result[n_out:]


def load(flags, ahead, behind):
    def kernel(flag_ref, in_refs, out_refs, scratch_refs):
        out_refs[0][...] = jnp.full((8, 128), flag_ref[0], jnp.int32)

    (done,), pieces = call(
        kernel,
        "load",
        flags,
        [],
        [jax.ShapeDtypeStruct((8, 128), jnp.int32)],
        ahead,
        [],
        0,
        behind,
    )
    return done, pieces


def attend(lengths, queries, keys, values, new_keys, new_values, resid):
    count, width = queries.shape
    cached = keys.shape[1]
    heads = width // HD
    groups = heads // KVH
    score_scale = 1.0 / HD**0.5
    inputs = (lengths, queries, keys, new_keys, values, new_values, resid)

    def kernel(*refs):
        slow_refs, refs = refs[: len(inputs)], refs[len(inputs) :]
        mixed_ref, square_ref, *fast_refs, sems = refs
        length_ref, q_ref, k_ref, kn_ref, v_ref, vn_ref, resid_ref = fast_refs
        copies = [
            pltpu.make_async_copy(slow, fast, sems.at[i])
            for i, (slow, fast) in enumerate(zip(slow_refs, fast_refs, strict=True))
        ]
        for copy in copies:
            copy.start()
        position = lax.broadcasted_iota(jnp.int32, (heads, cached), 1)

        def rows_of(ref, b):
            row = ref[b : b + 1, :].astype(F32)
            return jnp.concatenate(
                [
                    jnp.broadcast_to(row[:, g * HD : (g + 1) * HD], (groups, HD))
                    for g in range(KVH)
                ],
                axis=0,
            )

        for copy in copies[:4]:
            copy.wait()
        weights = []
        for b in range(count):
            q = q_ref[b : b + 1, :].astype(F32).reshape(heads, HD)
            q_narrow = q.astype(BF16)
            scores = [
                lax.dot_general(
                    q_narrow[g * groups : (g + 1) * groups],
                    k_ref[b, :, g * HD : (g + 1) * HD],
                    (((1,), (1,)), ((), ())),
                    preferred_element_type=F32,
                )
                for g in range(KVH)
            ]
            scores = jnp.concatenate(scores, axis=0) * score_scale
            own = jnp.sum(q * rows_of(kn_ref, b), axis=-1, keepdims=True) * score_scale
            live = position < length_ref[b]
            scores = jnp.where(live, scores, jnp.float32(-1e30))
            top = jnp.maximum(jnp.max(scores, axis=-1, keepdims=True), own)
            cache_exp = jnp.where(live, jnp.exp(scores - top), jnp.float32(0.0))
            own_exp = jnp.exp(own - top)
            total = jnp.sum(cache_exp, axis=-1, keepdims=True) + own_exp
            weights.append(
                ((cache_exp / total).astype(BF16), (own_exp / total).astype(BF16).astype(F32))
            )
        for copy in copies[4:]:
            copy.wait()
        for b in range(count):
            probs, own_prob = weights[b]
            attended = [
                jnp.dot(
                    probs[g * groups : (g + 1) * groups],
                    v_ref[b, :, g * HD : (g + 1) * HD],
                    preferred_element_type=F32,
                )
                for g in range(KVH)
            ]
            mixed = jnp.concatenate(attended, axis=0) + own_prob * rows_of(vn_ref, b)
            mixed = mixed + resid_ref[b : b + 1, :].astype(F32).reshape(heads, HD)
            mean_square = jnp.sum(mixed * mixed, keepdims=True) * (1.0 / width)
            mixed_ref[b : b + 1, :] = mixed.reshape(1, width)
            square_ref[b : b + 1, :] = jnp.broadcast_to(mean_square, (1, HD))

    fast = [pltpu.VMEM(x.shape, x.dtype) for x in inputs]
    fast[0] = pltpu.SMEM(lengths.shape, lengths.dtype)
    return pl.pallas_call(
        kernel,
        in_specs=[SLOW] * len(inputs),
        out_specs=[FAST, FAST],
        out_shape=[
            jax.ShapeDtypeStruct((count, width), F32),
            jax.ShapeDtypeStruct((count, HD), F32),
        ],
        scratch_shapes=[*fast, pltpu.SemaphoreType.DMA((len(inputs),))],
        compiler_params=pltpu.CompilerParams(vmem_limit_bytes=16 << 20),
        name="attend",
    )(*[pltpu.with_memory_space_constraint(x, pltpu.HBM) for x in inputs])


def gate_up(core, x, gates, ups, ahead, behind):
    rows, depth = x.shape
    half = rows // 2
    n, tile = len(gates), gates[0].shape[1]

    def kernel(core_ref, in_refs, out_refs, scratch_refs):
        x_ref, w_refs = in_refs[0], (in_refs[1 : n + 1], in_refs[n + 1 :])
        keep_ref, send_ref = out_refs
        upper = core_ref[0] == 0
        for j in range(n):
            at = slice(j * tile, (j + 1) * tile)
            for i in range(2):
                part = jnp.dot(x_ref[...], w_refs[i][j][...], preferred_element_type=F32)
                keep_ref[i, :, at] = jnp.where(upper, part[:half], part[half:])
                send_ref[i, :, at] = jnp.where(upper, part[half:], part[:half]).astype(BF16)

    return call(
        kernel,
        "gate_up",
        core,
        [x, *gates, *ups],
        [
            jax.ShapeDtypeStruct((2, half, n * tile), F32),
            jax.ShapeDtypeStruct((2, half, n * tile), BF16),
        ],
        ahead,
        [],
        4 * rows * depth * n * tile,
        behind,
    )


def down(core, mine, theirs, sums, weights, first, count, tile, split, ahead, behind):
    half = mine[0].shape[0]
    widths = [t.shape[1] for t in mine]
    n = len(mine)
    shapes = jax.eval_shape(split, jax.ShapeDtypeStruct((2 * half, tile), F32))
    with_sums = [] if sums is None else [sums]

    def kernel(core_ref, in_refs, out_refs, scratch_refs):
        (h_ref,) = scratch_refs
        own = pl.multiple_of(core_ref[0] * half, half)
        other = pl.multiple_of(half - core_ref[0] * half, half)
        at = 0
        for i in range(n):
            h_ref[pl.ds(own, half), at : at + widths[i]] = in_refs[i][...]
            h_ref[pl.ds(other, half), at : at + widths[i]] = in_refs[n + i][...]
            at += widths[i]
        for j in range(count):
            columns = slice((first + j) * tile, (first + j + 1) * tile)
            value, at = None, 0
            for i in range(n):
                term = jnp.dot(
                    h_ref[:, at : at + widths[i]],
                    in_refs[2 * n + i][:, columns],
                    preferred_element_type=F32,
                )
                value = term if value is None else value + term
                at += widths[i]
            for ref in in_refs[3 * n :]:
                value = value + ref[:, columns]
            for ref, part in zip(out_refs, split(value), strict=True):
                ref[:, j * tile : (j + 1) * tile] = part

    return call(
        kernel,
        "down",
        core,
        [*mine, *theirs, *weights, *with_sums],
        [jax.ShapeDtypeStruct((s.shape[0], count * tile), s.dtype) for s in shapes],
        ahead,
        [pltpu.VMEM((2 * half, sum(widths)), BF16)],
        4 * half * sum(widths) * count * tile,
        behind,
    )


def solution(mesh):
    n_wide, n_narrow = mesh.shape["wide"], mesh.shape["narrow"]
    n_far = n_wide // 2
    near_far = n_far // 2

    def narrow_swap(x, mask):
        return lax.ppermute(x, "narrow", [(i, i ^ mask) for i in range(n_narrow)])

    def wide_swap(x):
        return lax.ppermute(x, "wide", [(i, i ^ 1) for i in range(n_wide)])

    def far_swap(x, slot):
        return lax.ppermute(x, "wide", [(i, i ^ (slot << 1)) for i in range(n_wide)])

    def by_position(first, second):
        order = []
        for top in range(2):
            for side in (first, second):
                order += side[top * near_far : (top + 1) * near_far]
        return jnp.concatenate(order, axis=0)

    def from_narrow(pieces, am, j):
        out = pieces[j]
        for i in range(1, n_narrow):
            out = jnp.where(am[i], pieces[j ^ i], out)
        return out

    def body(
        resid,
        queries,
        key_cache,
        value_cache,
        new_keys,
        new_values,
        lengths,
        norm_gain,
        w_gate,
        w_up,
        w_down,
    ):
        own_rows = resid.shape[0]
        block = w_gate.shape[0]
        me = lax.axis_index("narrow").astype(jnp.uint32)
        partner = [me ^ jnp.uint32(s) for s in range(n_narrow)]
        place = (
            [p * jnp.uint32(block) for p in partner],
            [p * jnp.uint32(own_rows) for p in partner],
            [me == jnp.uint32(i) for i in range(n_narrow)],
            (me & jnp.uint32(1)).astype(jnp.int32).reshape(1),
        )
        place, queries = lax.optimization_barrier((place, queries))
        column_at, row_at, am, core = place
        tile = tile_of(w_gate.shape[1])
        tiles = w_gate.shape[1] // tile
        chunks = [[0], *[list(range(i, min(i + 2, tiles))) for i in range(1, tiles, 2)]]
        gates, ups, downs = {}, {}, {}

        def gate_up_pieces(which):
            return [
                Piece(w, 0, w.shape[0], j * tile, tile) for j in which for w in (w_gate, w_up)
            ]

        def take(which, pieces):
            for i, j in enumerate(which):
                gates[j], ups[j] = pieces[2 * i], pieces[2 * i + 1]

        def bring(which, behind):
            done, pieces = load(core, gate_up_pieces(which), behind)
            take(which, pieces)
            return done

        def down_pieces(which):
            return [
                Piece(w_down, chunks[c][0] * tile, len(chunks[c]) * tile, 0, w_down.shape[1])
                for c in which
            ]

        mixed, mean_square = attend(
            lengths, queries, key_cache, value_cache, new_keys, new_values, resid
        )
        normed = (
            mixed * lax.rsqrt(mean_square[:, :1] + 1e-05) * norm_gain.astype(F32)
        ).astype(BF16)
        def column_block(x, s):
            return lax.dynamic_slice(x, (jnp.uint32(0), column_at[s]), (own_rows, block))

        pieces = [column_block(normed, 0)]
        for s in range(1, n_narrow):
            pieces.append(narrow_swap(column_block(normed, s), s))
        group = jnp.concatenate([from_narrow(pieces, am, j) for j in range(n_narrow)], axis=0)
        group_rows = own_rows * n_narrow

        unit = tile_of(block)
        cut = (block // unit * 3 // 8) * unit
        left, right = group[:, :cut], group[:, cut:]
        pair = jnp.concatenate([left, wide_swap(left)], axis=0)
        far_right = [right] + [far_swap(right, s) for s in range(1, n_far)]
        first_done = bring([0, 1], [pair])
        pair = after(pair, far_right)
        far_pairs = [pair] + [far_swap(pair, s) for s in range(1, n_far)]
        other = wide_swap(jnp.concatenate(far_right, axis=0))
        second_done = bring([2, 3], [pair])
        far_pairs, other, second_done = lax.optimization_barrier((far_pairs, other, second_done))
        x_left = by_position(
            [p[:group_rows] for p in far_pairs], [p[group_rows:] for p in far_pairs]
        )
        x_right = by_position(
            far_right,
            [other[s * group_rows : (s + 1) * group_rows] for s in range(n_far)],
        )
        x = jnp.concatenate([x_left, x_right], axis=1)

        plan = [
            [],
            gate_up_pieces(chunks[2][1:]),
            gate_up_pieces(chunks[3]),
            down_pieces([0, 1]),
        ]
        chips, arrived, mine, theirs = [], [], [], []

        def finish(c):
            total = chips[c]
            for part in arrived[c]:
                total = total + part.astype(F32)
            hidden = (jax.nn.silu(total[0]) * total[1]).astype(BF16)
            mine.append(hidden)
            theirs.append(narrow_swap(hidden, 1))

        for c, which in enumerate(chunks):
            behind = [sent] if c else [first_done, second_done]
            (keep, send), pieces = gate_up(
                core, x, [gates[j] for j in which], [ups[j] for j in which], plan[c], behind
            )
            if c == 1:
                take(chunks[2][1:], pieces)
            elif c == 2:
                take(chunks[3], pieces)
            elif c == 3:
                downs[0], downs[1] = pieces
            if c:
                send, arrived[-1] = lax.optimization_barrier((send, arrived[-1]))
                finish(c - 1)
            chip = keep + narrow_swap(send, 1).astype(F32)
            sent = chip.astype(BF16)
            if c == len(chunks) - 1:
                sent, theirs[:2] = lax.optimization_barrier((sent, theirs[:2]))
            chips.append(chip)
            arrived.append([narrow_swap(sent, s) for s in range(2, n_narrow, 2)])

        column_tile = tile_of(w_down.shape[1])
        column_tiles = w_down.shape[1] // column_tile
        sums = None
        for low, high in ((0, 2), (2, 3)):
            (sums,), pieces = down(
                core,
                mine[low:high],
                theirs[low:high],
                sums,
                [downs[i] for i in range(low, high)],
                0,
                column_tiles,
                column_tile,
                lambda value: (value,),
                down_pieces([2, 3]) if low == 0 else [],
                [],
            )
            if low == 0:
                downs[2], downs[3] = pieces
        sums, arrived[-1] = lax.optimization_barrier((sums, arrived[-1]))
        finish(len(chunks) - 1)

        near_tiles = column_tiles * 5 // 8
        run = near_far * group_rows

        def split_near(value):
            kept = [value[2 * top * run : (2 * top + 1) * run] for top in range(2)]
            sent = [value[(2 * top + 1) * run : (2 * top + 2) * run] for top in range(2)]
            return jnp.concatenate(kept, axis=0), jnp.concatenate(sent, axis=0).astype(BF16)

        def split_far(value):
            out = []
            for top in range(2):
                for low in range(near_far):
                    at = 2 * top * run + low * group_rows
                    both = [value[i : i + group_rows] for i in (at, at + run)]
                    out.append(jnp.concatenate(both, axis=0))
            return (out[0], *[part.astype(BF16) for part in out[1:]])

        (kept, sent), _ = down(
            core,
            mine[3:],
            theirs[3:],
            sums,
            [downs[3]],
            0,
            near_tiles,
            column_tile,
            split_near,
            [],
            [],
        )
        far_parts, _ = down(
            core,
            mine[3:],
            theirs[3:],
            sums,
            [downs[3]],
            near_tiles,
            column_tiles - near_tiles,
            column_tile,
            split_far,
            [],
            [sent],
        )
        near_sum = kept + wide_swap(sent).astype(F32)
        near_sent = near_sum.astype(BF16)
        left_sum = near_sum[:group_rows]
        right_parts = [far_swap(far_parts[s], s) for s in range(1, n_far)]
        left_parts = [
            far_swap(near_sent[s * group_rows : (s + 1) * group_rows], s) for s in range(1, n_far)
        ]
        right_parts, left_parts[0] = lax.optimization_barrier((right_parts, left_parts[0]))
        right_sum = far_parts[0]
        for part in right_parts:
            right_sum = right_sum + part.astype(F32)
        for part in left_parts:
            left_sum = left_sum + part.astype(F32)
        right_sum = right_sum[:group_rows] + wide_swap(
            right_sum[group_rows:].astype(BF16)
        ).astype(F32)
        reduced = jnp.concatenate([left_sum, right_sum], axis=1).astype(BF16)

        def row_block(x, s):
            return lax.dynamic_slice(x, (row_at[s], jnp.uint32(0)), (own_rows, block))

        pieces = [row_block(reduced, 0)]
        for s in range(1, n_narrow):
            pieces.append(narrow_swap(row_block(reduced, s), s))
        ffn_out = jnp.concatenate([from_narrow(pieces, am, j) for j in range(n_narrow)], axis=1)
        return (mixed + ffn_out.astype(F32)).astype(BF16)

    return jax.shard_map(
        body,
        mesh=mesh,
        in_specs=(
            P(("wide", "narrow"), None),
            P(("wide", "narrow"), None),
            P(("wide", "narrow"), None, None),
            P(("wide", "narrow"), None, None),
            P(("wide", "narrow"), None),
            P(("wide", "narrow"), None),
            P(("wide", "narrow")),
            P(),
            P("narrow", "wide"),
            P("narrow", "wide"),
            P("wide", "narrow"),
        ),
        out_specs=P(("wide", "narrow"), None),
        check_vma=False,
    )
```

```python
import jax
import jax.numpy as jnp
from jax import lax
from jax.experimental import pallas as pl
from jax.experimental.pallas import tpu as pltpu
from jax.sharding import PartitionSpec as P

HEADS = 128
KVH = 8
HD = 128
F32 = jnp.float32
BF16 = jnp.bfloat16
COST = 16
SCOPED = 3 << 20
def tile_of(width):
    for tile in (512, 256, 128):
        if width % tile == 0:
            return tile
    return width


def after(x, *others):
    return lax.optimization_barrier((x, *others))[0]


SCALAR = pl.BlockSpec(memory_space=pltpu.SMEM)
FAST = pl.BlockSpec(memory_space=pltpu.VMEM)
SLOW = pl.BlockSpec(memory_space=pltpu.HBM)
ANY = pl.BlockSpec(memory_space=pl.ANY)


class Piece:
    def __init__(self, weight, row, rows, column, columns):
        self.weight = weight
        self.row, self.rows, self.column, self.columns = row, rows, column, columns


def call(kernel, name, flags, inputs, outputs, ahead, scratch, flops, behind):
    weights = []
    for piece in ahead:
        if not any(piece.weight is w for w in weights):
            weights.append(piece.weight)
    source = [next(i for i, w in enumerate(weights) if w is p.weight) for p in ahead]
    n_in, n_w, n_out, n_a = len(inputs), len(weights), len(outputs), len(ahead)

    def whole(*refs):
        flag_ref, refs = refs[0], refs[1:]
        in_refs, refs = refs[:n_in], refs[n_in + len(behind) :]
        weight_refs, refs = refs[:n_w], refs[n_w:]
        out_refs, refs = refs[:n_out], refs[n_out:]
        ahead_refs, refs = refs[:n_a], refs[n_a:]
        sems, scratch_refs = refs[0], refs[1:]
        copies = []
        for i, piece in enumerate(ahead):
            view = weight_refs[source[i]].at[
                pl.ds(piece.row, piece.rows), pl.ds(piece.column, piece.columns)
            ]
            copies.append(pltpu.make_async_copy(view, ahead_refs[i], sems.at[i]))
        for copy in copies:
            copy.start()
        kernel(flag_ref, in_refs, out_refs, scratch_refs)
        for copy in copies:
            copy.wait()

    moved = sum(2 * p.rows * p.columns for p in ahead)
    result = pl.pallas_call(
        whole,
        in_specs=[SCALAR, *[FAST] * n_in, *[ANY] * len(behind), *[SLOW] * n_w],
        out_specs=[FAST] * (n_out + n_a),
        out_shape=[*outputs, *[jax.ShapeDtypeStruct((p.rows, p.columns), BF16) for p in ahead]],
        scratch_shapes=[pltpu.SemaphoreType.DMA((max(1, n_a),)), *scratch],
        compiler_params=pltpu.CompilerParams(vmem_limit_bytes=SCOPED),
        cost_estimate=pl.CostEstimate(
            flops=flops // COST, bytes_accessed=moved // COST, transcendentals=0
        ),
        name=name,
    )(flags, *inputs, *behind, *[pltpu.with_memory_space_constraint(w, pltpu.HBM) for w in weights])
    return result[:n_out], result[n_out:]


def load(flags, ahead, behind):
    def kernel(flag_ref, in_refs, out_refs, scratch_refs):
        out_refs[0][...] = jnp.full((8, 128), flag_ref[0], jnp.int32)

    (done,), pieces = call(
        kernel,
        "load",
        flags,
        [],
        [jax.ShapeDtypeStruct((8, 128), jnp.int32)],
        ahead,
        [],
        0,
        behind,
    )
    return done, pieces


def attend(lengths, queries, keys, values, new_keys, new_values, resid, gain):
    count, width = queries.shape
    cached = keys.shape[1]
    heads = width // HD
    groups = heads // KVH
    score_scale = 1.0 / HD**0.5
    inputs = (lengths, queries, keys, new_keys, values, new_values, resid)

    def kernel(*refs):
        slow_refs, gain_ref, refs = refs[: len(inputs)], refs[len(inputs)], refs[len(inputs) + 1 :]
        mixed_ref, square_ref, gain_out, *fast_refs, sems = refs
        length_ref, q_ref, k_ref, kn_ref, v_ref, vn_ref, resid_ref = fast_refs
        copies = [
            pltpu.make_async_copy(slow, fast, sems.at[i])
            for i, (slow, fast) in enumerate(zip(slow_refs, fast_refs, strict=True))
        ]
        copies.append(pltpu.make_async_copy(gain_ref, gain_out, sems.at[len(inputs)]))
        for copy in copies:
            copy.start()
        position = lax.broadcasted_iota(jnp.int32, (heads, cached), 1)

        def rows_of(ref, b):
            row = ref[b : b + 1, :].astype(F32)
            return jnp.concatenate(
                [
                    jnp.broadcast_to(row[:, g * HD : (g + 1) * HD], (groups, HD))
                    for g in range(KVH)
                ],
                axis=0,
            )

        for copy in copies[:4]:
            copy.wait()
        weights = []
        for b in range(count):
            q = q_ref[b : b + 1, :].astype(F32).reshape(heads, HD)
            q_narrow = q.astype(BF16)
            scores = [
                lax.dot_general(
                    q_narrow[g * groups : (g + 1) * groups],
                    k_ref[b, :, g * HD : (g + 1) * HD],
                    (((1,), (1,)), ((), ())),
                    preferred_element_type=F32,
                )
                for g in range(KVH)
            ]
            scores = jnp.concatenate(scores, axis=0) * score_scale
            own = jnp.sum(q * rows_of(kn_ref, b), axis=-1, keepdims=True) * score_scale
            live = position < length_ref[b]
            scores = jnp.where(live, scores, jnp.float32(-1e30))
            top = jnp.maximum(jnp.max(scores, axis=-1, keepdims=True), own)
            cache_exp = jnp.where(live, jnp.exp(scores - top), jnp.float32(0.0))
            own_exp = jnp.exp(own - top)
            total = jnp.sum(cache_exp, axis=-1, keepdims=True) + own_exp
            weights.append(
                ((cache_exp / total).astype(BF16), (own_exp / total).astype(BF16).astype(F32))
            )
        for copy in copies[4:]:
            copy.wait()
        for b in range(count):
            probs, own_prob = weights[b]
            attended = [
                jnp.dot(
                    probs[g * groups : (g + 1) * groups],
                    v_ref[b, :, g * HD : (g + 1) * HD],
                    preferred_element_type=F32,
                )
                for g in range(KVH)
            ]
            mixed = jnp.concatenate(attended, axis=0) + own_prob * rows_of(vn_ref, b)
            mixed = mixed + resid_ref[b : b + 1, :].astype(F32).reshape(heads, HD)
            mean_square = jnp.sum(mixed * mixed, keepdims=True) * (1.0 / width)
            mixed_ref[b : b + 1, :] = mixed.reshape(1, width)
            square_ref[b : b + 1, :] = jnp.broadcast_to(mean_square, (1, HD))

    fast = [pltpu.VMEM(x.shape, x.dtype) for x in inputs]
    fast[0] = pltpu.SMEM(lengths.shape, lengths.dtype)
    return pl.pallas_call(
        kernel,
        in_specs=[SLOW] * (len(inputs) + 1),
        out_specs=[FAST] * 3,
        out_shape=[
            jax.ShapeDtypeStruct((count, width), F32),
            jax.ShapeDtypeStruct((count, HD), F32),
            jax.ShapeDtypeStruct(gain.shape, gain.dtype),
        ],
        scratch_shapes=[*fast, pltpu.SemaphoreType.DMA((len(inputs) + 1,))],
        compiler_params=pltpu.CompilerParams(vmem_limit_bytes=16 << 20),
        name="attend",
    )(*[pltpu.with_memory_space_constraint(x, pltpu.HBM) for x in (*inputs, gain)])


def gate_up(core, x, gates, ups, ahead, behind, places=None):
    depth = gates[0].shape[0]
    pieces = [x] if places is None else x
    rows = x.shape[0] if places is None else sum(p.size for p in pieces) // depth
    half = rows // 2
    m = len(pieces)
    made = [] if places is None else [jax.ShapeDtypeStruct((rows, depth), BF16)]
    n, tile = len(gates), gates[0].shape[1]

    def kernel(core_ref, in_refs, out_refs, scratch_refs):
        x_ref, w_refs = in_refs[0], (in_refs[m : n + m], in_refs[n + m :])
        *made_refs, keep_ref, send_ref = out_refs
        for x_ref in made_refs:
            for i in range(m):
                for source, count, row, column in places[i]:
                    x_ref[row : row + count, column : column + pieces[i].shape[1]] = in_refs[i][
                        source : source + count, :
                    ]
        upper = core_ref[0] == 0
        for j in range(n):
            at = slice(j * tile, (j + 1) * tile)
            for i in range(2):
                part = jnp.dot(x_ref[...], w_refs[i][j][...], preferred_element_type=F32)
                keep_ref[i, :, at] = jnp.where(upper, part[:half], part[half:])
                send_ref[i, :, at] = jnp.where(upper, part[half:], part[:half]).astype(BF16)

    return call(
        kernel,
        "gate_up",
        core,
        [*pieces, *gates, *ups],
        [
            *made,
            jax.ShapeDtypeStruct((2, half, n * tile), F32),
            jax.ShapeDtypeStruct((2, half, n * tile), BF16),
        ],
        ahead,
        [],
        4 * rows * depth * n * tile,
        behind,
    )


def down(core, mine, theirs, sums, weights, first, count, tile, split, ahead, behind):
    half = mine[0].shape[0]
    widths = [t.shape[1] for t in mine]
    n = len(mine)
    shapes = jax.eval_shape(split, jax.ShapeDtypeStruct((2 * half, tile), F32))
    with_sums = [] if sums is None else [sums]

    def kernel(core_ref, in_refs, out_refs, scratch_refs):
        (h_ref,) = scratch_refs
        own = pl.multiple_of(core_ref[0] * half, half)
        other = pl.multiple_of(half - core_ref[0] * half, half)
        at = 0
        for i in range(n):
            h_ref[pl.ds(own, half), at : at + widths[i]] = in_refs[i][...]
            h_ref[pl.ds(other, half), at : at + widths[i]] = in_refs[n + i][...]
            at += widths[i]
        for j in range(count):
            columns = slice((first + j) * tile, (first + j + 1) * tile)
            value, at = None, 0
            for i in range(n):
                term = jnp.dot(
                    h_ref[:, at : at + widths[i]],
                    in_refs[2 * n + i][:, columns],
                    preferred_element_type=F32,
                )
                value = term if value is None else value + term
                at += widths[i]
            for ref in in_refs[3 * n :]:
                value = value + ref[:, columns]
            for ref, part in zip(out_refs, split(value), strict=True):
                ref[:, j * tile : (j + 1) * tile] = part

    return call(
        kernel,
        "down",
        core,
        [*mine, *theirs, *weights, *with_sums],
        [jax.ShapeDtypeStruct((s.shape[0], count * tile), s.dtype) for s in shapes],
        ahead,
        [pltpu.VMEM((2 * half, sum(widths)), BF16)],
        4 * half * sum(widths) * count * tile,
        behind,
    )


def solution(mesh):
    n_wide, n_narrow = mesh.shape["wide"], mesh.shape["narrow"]
    n_far = n_wide // 2
    near_far = n_far // 2

    def narrow_swap(x, mask):
        return lax.ppermute(x, "narrow", [(i, i ^ mask) for i in range(n_narrow)])

    def wide_swap(x):
        return lax.ppermute(x, "wide", [(i, i ^ 1) for i in range(n_wide)])

    def far_swap(x, slot):
        return lax.ppermute(x, "wide", [(i, i ^ (slot << 1)) for i in range(n_wide)])

    def from_narrow(pieces, am, j):
        out = pieces[j]
        for i in range(1, n_narrow):
            out = jnp.where(am[i], pieces[j ^ i], out)
        return out

    def body(
        resid,
        queries,
        key_cache,
        value_cache,
        new_keys,
        new_values,
        lengths,
        norm_gain,
        w_gate,
        w_up,
        w_down,
    ):
        own_rows = resid.shape[0]
        block = w_gate.shape[0]
        me = lax.axis_index("narrow").astype(jnp.uint32)
        partner = [me ^ jnp.uint32(s) for s in range(n_narrow)]
        place = (
            [p * jnp.uint32(block) for p in partner],
            [p * jnp.uint32(own_rows) for p in partner],
            [me == jnp.uint32(i) for i in range(n_narrow)],
            (me & jnp.uint32(1)).astype(jnp.int32).reshape(1),
        )
        place, queries = lax.optimization_barrier((place, queries))
        column_at, row_at, am, core = place
        tile = tile_of(w_gate.shape[1])
        tiles = w_gate.shape[1] // tile
        middle = 1 + tiles // 2
        chunks = [[0], list(range(1, middle)), list(range(middle, tiles))]
        gates, ups, downs = {}, {}, {}

        def gate_up_pieces(which):
            return [
                Piece(w, 0, w.shape[0], j * tile, tile) for j in which for w in (w_gate, w_up)
            ]

        def take(which, pieces):
            for i, j in enumerate(which):
                gates[j], ups[j] = pieces[2 * i], pieces[2 * i + 1]

        def bring(which, behind):
            done, pieces = load(core, gate_up_pieces(which), behind)
            take(which, pieces)
            return done

        early = chunks[1] + chunks[2][:1]
        def down_pieces(which):
            return [
                Piece(w_down, chunks[c][0] * tile, len(chunks[c]) * tile, 0, w_down.shape[1])
                for c in which
            ]

        mixed, mean_square, gain = attend(
            lengths, queries, key_cache, value_cache, new_keys, new_values, resid, norm_gain
        )
        normed = (
            mixed * lax.rsqrt(mean_square[:, :1] + 1e-05) * gain.astype(F32)
        ).astype(BF16)
        def column_block(x, s):
            return lax.dynamic_slice(x, (jnp.uint32(0), column_at[s]), (own_rows, block))

        pieces = [column_block(normed, 0)]
        for s in range(1, n_narrow):
            pieces.append(narrow_swap(column_block(normed, s), s))
        done = bring(chunks[0], [normed])
        pieces, first_done = lax.optimization_barrier((pieces, done))
        group = jnp.concatenate([from_narrow(pieces, am, j) for j in range(n_narrow)], axis=0)
        group_rows = own_rows * n_narrow

        unit = tile_of(block)
        cut = (block // unit * 3 // 8) * unit
        left, right = group[:, :cut], group[:, cut:]
        pair = jnp.concatenate([left, wide_swap(left)], axis=0)
        far_right = [right] + [far_swap(right, s) for s in range(1, n_far)]
        done = bring(early[: len(early) // 2], [pair])
        pair, far_right, done = lax.optimization_barrier((pair, far_right, done))
        other = wide_swap(jnp.concatenate(far_right, axis=0))
        far_pairs = [pair] + [far_swap(pair, s) for s in range(1, n_far)]
        second_done = bring(early[len(early) // 2 :], [pair])
        far_pairs, other, second_done = lax.optimization_barrier((far_pairs, other, second_done))

        run = near_far * group_rows

        def row_of(far, near):
            return (2 * (far // near_far) + near) * run + far % near_far * group_rows

        x_pieces = [*far_pairs, *far_right, other]
        places = [
            *[
                [(side * group_rows, group_rows, row_of(s, side), 0) for side in range(2)]
                for s in range(n_far)
            ],
            *[[(0, group_rows, row_of(s, 0), cut)] for s in range(n_far)],
            [(s * group_rows, group_rows, row_of(s, 1), cut) for s in range(n_far)],
        ]

        plan = [[], gate_up_pieces(chunks[2][1:2]), down_pieces([0])]
        chips, arrived, mine, theirs = [], [], [], []

        def finish(c):
            total = chips[c]
            for part in arrived[c]:
                total = total + part.astype(F32)
            hidden = (jax.nn.silu(total[0]) * total[1]).astype(BF16)
            mine.append(hidden)

        for c, which in enumerate(chunks):
            behind = [sent] if c else [first_done, done, second_done]
            if c == 2:
                bring(chunks[2][2:], [sent])
            (*made, keep, send), pieces = gate_up(
                core,
                x if c else x_pieces,
                [gates[j] for j in which],
                [ups[j] for j in which],
                plan[c],
                behind,
                None if c else places,
            )
            if c == 0:
                (x,) = made
            elif c == 1:
                take(chunks[2][1:2], pieces)
            else:
                downs[0] = pieces[0]
            if c == 1:
                send, arrived[-1] = lax.optimization_barrier((send, arrived[-1]))
            chip = keep + narrow_swap(send, 1).astype(F32)
            sent = chip.astype(BF16)
            if c:
                finish(c - 1)
            if c > 1:
                sent, mine[c - 1] = lax.optimization_barrier((sent, mine[c - 1]))
            if c > 1:
                sent, theirs[0] = lax.optimization_barrier((sent, theirs[0]))
            if c:
                theirs.append(narrow_swap(mine[c - 1], 1))
            chips.append(chip)
            arrived.append([narrow_swap(sent, s) for s in range(2, n_narrow, 2)])

        column_tile = tile_of(w_down.shape[1])
        column_tiles = w_down.shape[1] // column_tile
        _, (downs[1],) = load(core, down_pieces([1]), [sent])
        (sums,), (downs[2],) = down(
            core,
            mine,
            theirs,
            None,
            [downs[0], downs[1]],
            0,
            column_tiles,
            column_tile,
            lambda value: (value,),
            down_pieces([2]),
            [],
        )
        sums, arrived[-1] = lax.optimization_barrier((sums, arrived[-1]))
        finish(len(chunks) - 1)
        theirs.append(narrow_swap(mine[-1], 1))

        near_tiles = column_tiles * 5 // 8
        def split_near(value):
            kept = [value[2 * top * run : (2 * top + 1) * run] for top in range(2)]
            sent = [value[(2 * top + 1) * run : (2 * top + 2) * run] for top in range(2)]
            return jnp.concatenate(kept, axis=0), jnp.concatenate(sent, axis=0).astype(BF16)

        def split_far(value):
            out = []
            for top in range(2):
                for low in range(near_far):
                    at = 2 * top * run + low * group_rows
                    both = [value[i : i + group_rows] for i in (at, at + run)]
                    out.append(jnp.concatenate(both, axis=0))
            return (out[0], *[part.astype(BF16) for part in out[1:]])

        (kept, sent), _ = down(
            core,
            mine[2:],
            theirs[2:],
            sums,
            [downs[2]],
            0,
            near_tiles,
            column_tile,
            split_near,
            [],
            [],
        )
        far_parts, _ = down(
            core,
            mine[2:],
            theirs[2:],
            sums,
            [downs[2]],
            near_tiles,
            column_tiles - near_tiles,
            column_tile,
            split_far,
            [],
            [sent],
        )
        near_sum = kept + wide_swap(sent).astype(F32)
        near_sent = near_sum.astype(BF16)
        left_sum = near_sum[:group_rows]
        right_parts = [far_swap(far_parts[s], s) for s in range(1, n_far)]
        left_parts = [
            far_swap(near_sent[s * group_rows : (s + 1) * group_rows], s) for s in range(1, n_far)
        ]
        right_parts, left_parts[0] = lax.optimization_barrier((right_parts, left_parts[0]))
        right_sum = far_parts[0]
        for part in right_parts:
            right_sum = right_sum + part.astype(F32)
        for part in left_parts:
            left_sum = left_sum + part.astype(F32)
        right_sum = right_sum[:group_rows] + wide_swap(
            right_sum[group_rows:].astype(BF16)
        ).astype(F32)
        reduced = jnp.concatenate([left_sum, right_sum], axis=1).astype(BF16)

        def row_block(x, s):
            return lax.dynamic_slice(x, (row_at[s], jnp.uint32(0)), (own_rows, block))

        pieces = [row_block(reduced, 0)]
        for s in range(1, n_narrow):
            pieces.append(narrow_swap(row_block(reduced, s), s))
        ffn_out = jnp.concatenate([from_narrow(pieces, am, j) for j in range(n_narrow)], axis=1)
        return (mixed + ffn_out.astype(F32)).astype(BF16)

    return jax.shard_map(
        body,
        mesh=mesh,
        in_specs=(
            P(("wide", "narrow"), None),
            P(("wide", "narrow"), None),
            P(("wide", "narrow"), None, None),
            P(("wide", "narrow"), None, None),
            P(("wide", "narrow"), None),
            P(("wide", "narrow"), None),
            P(("wide", "narrow")),
            P(),
            P("narrow", "wide"),
            P("narrow", "wide"),
            P("wide", "narrow"),
        ),
        out_specs=P(("wide", "narrow"), None),
        check_vma=False,
    )
```

```python
import jax
import jax.numpy as jnp
from jax import lax
from jax.experimental import pallas as pl
from jax.experimental.pallas import tpu as pltpu
from jax.sharding import PartitionSpec as P

HEADS = 128
KVH = 8
HD = 128
F32 = jnp.float32
BF16 = jnp.bfloat16
COST = 16
SCOPED = 3 << 20
def tile_of(width):
    for tile in (512, 256, 128):
        if width % tile == 0:
            return tile
    return width


def after(x, *others):
    return lax.optimization_barrier((x, *others))[0]


SCALAR = pl.BlockSpec(memory_space=pltpu.SMEM)
FAST = pl.BlockSpec(memory_space=pltpu.VMEM)
SLOW = pl.BlockSpec(memory_space=pltpu.HBM)
ANY = pl.BlockSpec(memory_space=pl.ANY)


class Piece:
    def __init__(self, weight, row, rows, column, columns):
        self.weight = weight
        self.row, self.rows, self.column, self.columns = row, rows, column, columns


def call(kernel, name, flags, inputs, outputs, ahead, scratch, flops, behind, late=()):
    moving = (*late, *ahead)
    weights = []
    for piece in moving:
        if not any(piece.weight is w for w in weights):
            weights.append(piece.weight)
    source = [next(i for i, w in enumerate(weights) if w is p.weight) for p in moving]
    n_in, n_w, n_out, n_a = len(inputs), len(weights), len(outputs), len(ahead)
    n_late = len(late)

    def whole(*refs):
        flag_ref, refs = refs[0], refs[1:]
        in_refs, refs = refs[:n_in], refs[n_in + len(behind) :]
        weight_refs, refs = refs[:n_w], refs[n_w:]
        out_refs, refs = refs[:n_out], refs[n_out:]
        ahead_refs, refs = refs[:n_a], refs[n_a:]
        sems, refs = refs[0], refs[1:]
        late_refs, scratch_refs = refs[:n_late], refs[n_late:]
        targets = (*late_refs, *ahead_refs)
        copies = []
        for i, piece in enumerate(moving):
            view = weight_refs[source[i]].at[
                pl.ds(piece.row, piece.rows), pl.ds(piece.column, piece.columns)
            ]
            copies.append(pltpu.make_async_copy(view, targets[i], sems.at[i]))
        for copy in copies:
            copy.start()
        if late:
            kernel(flag_ref, in_refs, out_refs, scratch_refs, late_refs, copies[:n_late])
        else:
            kernel(flag_ref, in_refs, out_refs, scratch_refs)
        for copy in copies[n_late:]:
            copy.wait()

    moved = sum(2 * p.rows * p.columns for p in moving)
    own = sum(2 * p.rows * p.columns for p in late)
    result = pl.pallas_call(
        whole,
        in_specs=[SCALAR, *[FAST] * n_in, *[ANY] * len(behind), *[SLOW] * n_w],
        out_specs=[FAST] * (n_out + n_a),
        out_shape=[*outputs, *[jax.ShapeDtypeStruct((p.rows, p.columns), BF16) for p in ahead]],
        scratch_shapes=[
            pltpu.SemaphoreType.DMA((max(1, len(moving)),)),
            *[pltpu.VMEM((p.rows, p.columns), BF16) for p in late],
            *scratch,
        ],
        compiler_params=pltpu.CompilerParams(vmem_limit_bytes=SCOPED + own),
        cost_estimate=pl.CostEstimate(
            flops=flops // COST, bytes_accessed=moved // COST, transcendentals=0
        ),
        name=name,
    )(flags, *inputs, *behind, *[pltpu.with_memory_space_constraint(w, pltpu.HBM) for w in weights])
    return result[:n_out], result[n_out:]


def load(flags, ahead, behind):
    def kernel(flag_ref, in_refs, out_refs, scratch_refs):
        out_refs[0][...] = jnp.full((8, 128), flag_ref[0], jnp.int32)

    (done,), pieces = call(
        kernel,
        "load",
        flags,
        [],
        [jax.ShapeDtypeStruct((8, 128), jnp.int32)],
        ahead,
        [],
        0,
        behind,
    )
    return done, pieces


def attend(lengths, queries, keys, values, new_keys, new_values, resid, gain):
    count, width = queries.shape
    cached = keys.shape[1]
    heads = width // HD
    groups = heads // KVH
    score_scale = 1.0 / HD**0.5
    inputs = (lengths, queries, keys, new_keys, values, new_values, resid)

    def kernel(*refs):
        slow_refs, gain_ref, refs = refs[: len(inputs)], refs[len(inputs)], refs[len(inputs) + 1 :]
        mixed_ref, square_ref, gain_out, *fast_refs, sems = refs
        length_ref, q_ref, k_ref, kn_ref, v_ref, vn_ref, resid_ref = fast_refs
        copies = [
            pltpu.make_async_copy(slow, fast, sems.at[i])
            for i, (slow, fast) in enumerate(zip(slow_refs, fast_refs, strict=True))
        ]
        copies.append(pltpu.make_async_copy(gain_ref, gain_out, sems.at[len(inputs)]))
        for copy in copies:
            copy.start()
        position = lax.broadcasted_iota(jnp.int32, (heads, cached), 1)
        owner = lax.broadcasted_iota(jnp.int32, (heads, HD), 0) // groups

        def rows_of(ref, b):
            row = ref[b : b + 1, :].astype(F32)
            return jnp.concatenate(
                [
                    jnp.broadcast_to(row[:, g * HD : (g + 1) * HD], (groups, HD))
                    for g in range(KVH)
                ],
                axis=0,
            )

        for copy in copies[:4]:
            copy.wait()
        weights = []
        for b in range(count):
            q = q_ref[b : b + 1, :].astype(F32).reshape(heads, HD)
            spread = jnp.concatenate(
                [jnp.where(owner == g, q, 0.0).astype(BF16) for g in range(KVH)], axis=1
            )
            scores = lax.dot_general(
                spread, k_ref[b], (((1,), (1,)), ((), ())), preferred_element_type=F32
            )
            scores = scores * score_scale
            own = jnp.sum(q * rows_of(kn_ref, b), axis=-1, keepdims=True) * score_scale
            live = position < length_ref[b]
            scores = jnp.where(live, scores, jnp.float32(-1e30))
            top = jnp.maximum(jnp.max(scores, axis=-1, keepdims=True), own)
            cache_exp = jnp.where(live, jnp.exp(scores - top), jnp.float32(0.0))
            own_exp = jnp.exp(own - top)
            total = jnp.sum(cache_exp, axis=-1, keepdims=True) + own_exp
            weights.append(
                ((cache_exp / total).astype(BF16), (own_exp / total).astype(BF16).astype(F32))
            )
        for copy in copies[4:]:
            copy.wait()
        for b in range(count):
            probs, own_prob = weights[b]
            product = jnp.dot(probs, v_ref[b], preferred_element_type=F32)
            attended = [
                product[g * groups : (g + 1) * groups, g * HD : (g + 1) * HD] for g in range(KVH)
            ]
            mixed = jnp.concatenate(attended, axis=0) + own_prob * rows_of(vn_ref, b)
            mixed = mixed + resid_ref[b : b + 1, :].astype(F32).reshape(heads, HD)
            mean_square = jnp.sum(mixed * mixed, keepdims=True) * (1.0 / width)
            mixed_ref[b : b + 1, :] = mixed.reshape(1, width)
            square_ref[b : b + 1, :] = jnp.broadcast_to(mean_square, (1, HD))

    fast = [pltpu.VMEM(x.shape, x.dtype) for x in inputs]
    fast[0] = pltpu.SMEM(lengths.shape, lengths.dtype)
    return pl.pallas_call(
        kernel,
        in_specs=[SLOW] * (len(inputs) + 1),
        out_specs=[FAST] * 3,
        out_shape=[
            jax.ShapeDtypeStruct((count, width), F32),
            jax.ShapeDtypeStruct((count, HD), F32),
            jax.ShapeDtypeStruct(gain.shape, gain.dtype),
        ],
        scratch_shapes=[*fast, pltpu.SemaphoreType.DMA((len(inputs) + 1,))],
        compiler_params=pltpu.CompilerParams(vmem_limit_bytes=16 << 20),
        name="attend",
    )(*[pltpu.with_memory_space_constraint(x, pltpu.HBM) for x in (*inputs, gain)])


def gate_up(core, x, gates, ups, ahead, behind, places=None, late=()):
    depth = gates[0].shape[0]
    pieces = [x] if places is None else x
    rows = x.shape[0] if places is None else sum(p.size for p in pieces) // depth
    half = rows // 2
    m = len(pieces)
    made = [] if places is None else [jax.ShapeDtypeStruct((rows, depth), BF16)]
    held, tile = len(gates), gates[0].shape[1]
    n = held + len(late) // 2

    def kernel(core_ref, in_refs, out_refs, scratch_refs, late_refs=(), copies=()):
        x_ref, w_refs = in_refs[0], (in_refs[m : held + m], in_refs[held + m :])
        *made_refs, keep_ref, send_ref = out_refs
        for x_ref in made_refs:
            for i in range(m):
                for source, count, row, column in places[i]:
                    x_ref[row : row + count, column : column + pieces[i].shape[1]] = in_refs[i][
                        source : source + count, :
                    ]
        upper = core_ref[0] == 0
        for j in range(n):
            at = slice(j * tile, (j + 1) * tile)
            for i in range(2):
                if j < held:
                    w_ref = w_refs[i][j]
                else:
                    w_ref = late_refs[2 * (j - held) + i]
                    copies[2 * (j - held) + i].wait()
                part = jnp.dot(x_ref[...], w_ref[...], preferred_element_type=F32)
                keep_ref[i, :, at] = jnp.where(upper, part[:half], part[half:])
                send_ref[i, :, at] = jnp.where(upper, part[half:], part[:half]).astype(BF16)

    return call(
        kernel,
        "gate_up",
        core,
        [*pieces, *gates, *ups],
        [
            *made,
            jax.ShapeDtypeStruct((2, half, n * tile), F32),
            jax.ShapeDtypeStruct((2, half, n * tile), BF16),
        ],
        ahead,
        [],
        4 * rows * depth * n * tile,
        behind,
        late,
    )


def down(core, mine, theirs, sums, weights, first, count, tile, split, ahead, behind):
    half = mine[0].shape[0]
    widths = [t.shape[1] for t in mine]
    n = len(mine)
    shapes = jax.eval_shape(split, jax.ShapeDtypeStruct((2 * half, tile), F32))
    with_sums = [] if sums is None else [sums]

    def kernel(core_ref, in_refs, out_refs, scratch_refs):
        (h_ref,) = scratch_refs
        own = pl.multiple_of(core_ref[0] * half, half)
        other = pl.multiple_of(half - core_ref[0] * half, half)
        at = 0
        for i in range(n):
            h_ref[pl.ds(own, half), at : at + widths[i]] = in_refs[i][...]
            h_ref[pl.ds(other, half), at : at + widths[i]] = in_refs[n + i][...]
            at += widths[i]
        for j in range(count):
            columns = slice((first + j) * tile, (first + j + 1) * tile)
            value, at = None, 0
            for i in range(n):
                term = jnp.dot(
                    h_ref[:, at : at + widths[i]],
                    in_refs[2 * n + i][:, columns],
                    preferred_element_type=F32,
                )
                value = term if value is None else value + term
                at += widths[i]
            for ref in in_refs[3 * n :]:
                value = value + ref[:, columns]
            for ref, part in zip(out_refs, split(value), strict=True):
                ref[:, j * tile : (j + 1) * tile] = part

    return call(
        kernel,
        "down",
        core,
        [*mine, *theirs, *weights, *with_sums],
        [jax.ShapeDtypeStruct((s.shape[0], count * tile), s.dtype) for s in shapes],
        ahead,
        [pltpu.VMEM((2 * half, sum(widths)), BF16)],
        4 * half * sum(widths) * count * tile,
        behind,
    )


def solution(mesh):
    n_wide, n_narrow = mesh.shape["wide"], mesh.shape["narrow"]
    n_far = n_wide // 2
    near_far = n_far // 2

    def narrow_swap(x, mask):
        return lax.ppermute(x, "narrow", [(i, i ^ mask) for i in range(n_narrow)])

    def wide_swap(x):
        return lax.ppermute(x, "wide", [(i, i ^ 1) for i in range(n_wide)])

    def far_swap(x, slot):
        return lax.ppermute(x, "wide", [(i, i ^ (slot << 1)) for i in range(n_wide)])

    def from_narrow(pieces, am, j):
        out = pieces[j]
        for i in range(1, n_narrow):
            out = jnp.where(am[i], pieces[j ^ i], out)
        return out

    def body(
        resid,
        queries,
        key_cache,
        value_cache,
        new_keys,
        new_values,
        lengths,
        norm_gain,
        w_gate,
        w_up,
        w_down,
    ):
        own_rows = resid.shape[0]
        block = w_gate.shape[0]
        me = lax.axis_index("narrow").astype(jnp.uint32)
        partner = [me ^ jnp.uint32(s) for s in range(n_narrow)]
        place = (
            [p * jnp.uint32(block) for p in partner],
            [p * jnp.uint32(own_rows) for p in partner],
            [me == jnp.uint32(i) for i in range(n_narrow)],
            (me & jnp.uint32(1)).astype(jnp.int32).reshape(1),
        )
        place, queries = lax.optimization_barrier((place, queries))
        column_at, row_at, am, core = place
        tile = tile_of(w_gate.shape[1])
        tiles = w_gate.shape[1] // tile
        middle = 1 + tiles // 2
        chunks = [[0], list(range(1, middle)), list(range(middle, tiles))]
        gates, ups, downs = {}, {}, {}

        def gate_up_pieces(which):
            return [
                Piece(w, 0, w.shape[0], j * tile, tile) for j in which for w in (w_gate, w_up)
            ]

        def take(which, pieces):
            for i, j in enumerate(which):
                gates[j], ups[j] = pieces[2 * i], pieces[2 * i + 1]

        def bring(which, behind):
            done, pieces = load(core, gate_up_pieces(which), behind)
            take(which, pieces)
            return done

        early = chunks[1] + chunks[2][:1]
        def down_pieces(which):
            return [
                Piece(w_down, chunks[c][0] * tile, len(chunks[c]) * tile, 0, w_down.shape[1])
                for c in which
            ]

        mixed, mean_square, gain = attend(
            lengths, queries, key_cache, value_cache, new_keys, new_values, resid, norm_gain
        )
        normed = (
            mixed * lax.rsqrt(mean_square[:, :1] + 1e-05) * gain.astype(F32)
        ).astype(BF16)
        def column_block(x, s):
            return lax.dynamic_slice(x, (jnp.uint32(0), column_at[s]), (own_rows, block))

        pieces = [column_block(normed, 0)]
        for s in range(1, n_narrow):
            pieces.append(narrow_swap(column_block(normed, s), s))
        done = bring(chunks[0], [normed])
        pieces, first_done = lax.optimization_barrier((pieces, done))
        group = jnp.concatenate([from_narrow(pieces, am, j) for j in range(n_narrow)], axis=0)
        group_rows = own_rows * n_narrow

        unit = tile_of(block)
        cut = (block // unit * 3 // 8) * unit
        left, right = group[:, :cut], group[:, cut:]
        pair = jnp.concatenate([left, wide_swap(left)], axis=0)
        far_right = [right] + [far_swap(right, s) for s in range(1, n_far)]
        done = bring(early[: len(early) // 2], [pair])
        pair, far_right, done = lax.optimization_barrier((pair, far_right, done))
        other = wide_swap(jnp.concatenate(far_right, axis=0))
        far_pairs = [pair] + [far_swap(pair, s) for s in range(1, n_far)]
        second_done = bring(early[len(early) // 2 :], [pair])
        far_pairs, other, second_done = lax.optimization_barrier((far_pairs, other, second_done))

        run = near_far * group_rows

        def row_of(far, near):
            return (2 * (far // near_far) + near) * run + far % near_far * group_rows

        x_pieces = [*far_pairs, *far_right, other]
        places = [
            *[
                [(side * group_rows, group_rows, row_of(s, side), 0) for side in range(2)]
                for s in range(n_far)
            ],
            *[[(0, group_rows, row_of(s, 0), cut)] for s in range(n_far)],
            [(s * group_rows, group_rows, row_of(s, 1), cut) for s in range(n_far)],
        ]

        plan = [[], [], down_pieces([0])]
        late = gate_up_pieces(chunks[2][1:])
        chips, arrived, mine, theirs = [], [], [], []

        def finish(c):
            total = chips[c]
            for part in arrived[c]:
                total = total + part.astype(F32)
            hidden = (jax.nn.silu(total[0]) * total[1]).astype(BF16)
            mine.append(hidden)

        for c, which in enumerate(chunks):
            behind = [sent] if c else [first_done, done, second_done]
            (*made, keep, send), pieces = gate_up(
                core,
                x if c else x_pieces,
                [gates[j] for j in which if j in gates],
                [ups[j] for j in which if j in ups],
                plan[c],
                behind,
                None if c else places,
                late if c == 2 else (),
            )
            if c == 0:
                (x,) = made
            elif c == 2:
                (downs[0],) = pieces
            chip = keep + narrow_swap(send, 1).astype(F32)
            sent = chip.astype(BF16)
            if c:
                finish(c - 1)
                sent, mine[c - 1] = lax.optimization_barrier((sent, mine[c - 1]))
            if c > 1:
                sent, theirs[0] = lax.optimization_barrier((sent, theirs[0]))
            if c:
                theirs.append(narrow_swap(mine[c - 1], 1))
            chips.append(chip)
            arrived.append([narrow_swap(sent, s) for s in range(2, n_narrow, 2)])

        column_tile = tile_of(w_down.shape[1])
        column_tiles = w_down.shape[1] // column_tile
        _, (downs[1],) = load(core, down_pieces([1]), [sent])
        (sums,), (downs[2],) = down(
            core,
            mine,
            theirs,
            None,
            [downs[0], downs[1]],
            0,
            column_tiles,
            column_tile,
            lambda value: (value,),
            down_pieces([2]),
            [],
        )
        sums, arrived[-1] = lax.optimization_barrier((sums, arrived[-1]))
        finish(len(chunks) - 1)
        theirs.append(narrow_swap(mine[-1], 1))

        near_tiles = column_tiles * 5 // 8
        def split_near(value):
            kept = [value[2 * top * run : (2 * top + 1) * run] for top in range(2)]
            sent = [value[(2 * top + 1) * run : (2 * top + 2) * run] for top in range(2)]
            return jnp.concatenate(kept, axis=0), jnp.concatenate(sent, axis=0).astype(BF16)

        def split_far(value):
            out = []
            for top in range(2):
                for low in range(near_far):
                    at = 2 * top * run + low * group_rows
                    both = [value[i : i + group_rows] for i in (at, at + run)]
                    out.append(jnp.concatenate(both, axis=0))
            return (out[0], *[part.astype(BF16) for part in out[1:]])

        (kept, sent), _ = down(
            core,
            mine[2:],
            theirs[2:],
            sums,
            [downs[2]],
            0,
            near_tiles,
            column_tile,
            split_near,
            [],
            [],
        )
        far_parts, _ = down(
            core,
            mine[2:],
            theirs[2:],
            sums,
            [downs[2]],
            near_tiles,
            column_tiles - near_tiles,
            column_tile,
            split_far,
            [],
            [sent],
        )
        near_sum = kept + wide_swap(sent).astype(F32)
        near_sent = near_sum.astype(BF16)
        left_sum = near_sum[:group_rows]
        right_parts = [far_swap(far_parts[s], s) for s in range(1, n_far)]
        left_parts = [
            far_swap(near_sent[s * group_rows : (s + 1) * group_rows], s) for s in range(1, n_far)
        ]
        right_parts, left_parts[0] = lax.optimization_barrier((right_parts, left_parts[0]))
        right_sum = far_parts[0]
        for part in right_parts:
            right_sum = right_sum + part.astype(F32)
        for part in left_parts:
            left_sum = left_sum + part.astype(F32)
        right_sum = right_sum[:group_rows] + wide_swap(
            right_sum[group_rows:].astype(BF16)
        ).astype(F32)
        reduced = jnp.concatenate([left_sum, right_sum], axis=1).astype(BF16)

        def row_block(x, s):
            return lax.dynamic_slice(x, (row_at[s], jnp.uint32(0)), (own_rows, block))

        pieces = [row_block(reduced, 0)]
        for s in range(1, n_narrow):
            pieces.append(narrow_swap(row_block(reduced, s), s))
        ffn_out = jnp.concatenate([from_narrow(pieces, am, j) for j in range(n_narrow)], axis=1)
        return (mixed + ffn_out.astype(F32)).astype(BF16)

    return jax.shard_map(
        body,
        mesh=mesh,
        in_specs=(
            P(("wide", "narrow"), None),
            P(("wide", "narrow"), None),
            P(("wide", "narrow"), None, None),
            P(("wide", "narrow"), None, None),
            P(("wide", "narrow"), None),
            P(("wide", "narrow"), None),
            P(("wide", "narrow")),
            P(),
            P("narrow", "wide"),
            P("narrow", "wide"),
            P("wide", "narrow"),
        ),
        out_specs=P(("wide", "narrow"), None),
        check_vma=False,
    )
```

```python
import jax
import jax.numpy as jnp
from jax import lax
from jax.experimental import pallas as pl
from jax.experimental.pallas import tpu as pltpu
from jax.sharding import PartitionSpec as P

HEADS = 128
KVH = 8
HD = 128
F32 = jnp.float32
BF16 = jnp.bfloat16
COST = 16
SCOPED = 3 << 20
def tile_of(width):
    for tile in (512, 256, 128):
        if width % tile == 0:
            return tile
    return width


def after(x, *others):
    return lax.optimization_barrier((x, *others))[0]


SCALAR = pl.BlockSpec(memory_space=pltpu.SMEM)
FAST = pl.BlockSpec(memory_space=pltpu.VMEM)
SLOW = pl.BlockSpec(memory_space=pltpu.HBM)
ANY = pl.BlockSpec(memory_space=pl.ANY)


class Piece:
    def __init__(self, weight, row, rows, column, columns):
        self.weight = weight
        self.row, self.rows, self.column, self.columns = row, rows, column, columns


def call(kernel, name, flags, inputs, outputs, ahead, scratch, flops, behind, late=()):
    moving = (*late, *ahead)
    weights = []
    for piece in moving:
        if not any(piece.weight is w for w in weights):
            weights.append(piece.weight)
    source = [next(i for i, w in enumerate(weights) if w is p.weight) for p in moving]
    n_in, n_w, n_out, n_a = len(inputs), len(weights), len(outputs), len(ahead)
    n_late = len(late)

    def whole(*refs):
        flag_ref, refs = refs[0], refs[1:]
        in_refs, refs = refs[:n_in], refs[n_in + len(behind) :]
        weight_refs, refs = refs[:n_w], refs[n_w:]
        out_refs, refs = refs[:n_out], refs[n_out:]
        ahead_refs, refs = refs[:n_a], refs[n_a:]
        sems, refs = refs[0], refs[1:]
        late_refs, scratch_refs = refs[:n_late], refs[n_late:]
        targets = (*late_refs, *ahead_refs)
        copies = []
        for i, piece in enumerate(moving):
            view = weight_refs[source[i]].at[
                pl.ds(piece.row, piece.rows), pl.ds(piece.column, piece.columns)
            ]
            copies.append(pltpu.make_async_copy(view, targets[i], sems.at[i]))
        for copy in copies:
            copy.start()
        if late:
            kernel(flag_ref, in_refs, out_refs, scratch_refs, late_refs, copies[:n_late])
        else:
            kernel(flag_ref, in_refs, out_refs, scratch_refs)
        for copy in copies[n_late:]:
            copy.wait()

    moved = sum(2 * p.rows * p.columns for p in moving)
    own = sum(2 * p.rows * p.columns for p in late)
    result = pl.pallas_call(
        whole,
        in_specs=[SCALAR, *[FAST] * n_in, *[ANY] * len(behind), *[SLOW] * n_w],
        out_specs=[FAST] * (n_out + n_a),
        out_shape=[*outputs, *[jax.ShapeDtypeStruct((p.rows, p.columns), BF16) for p in ahead]],
        scratch_shapes=[
            pltpu.SemaphoreType.DMA((max(1, len(moving)),)),
            *[pltpu.VMEM((p.rows, p.columns), BF16) for p in late],
            *scratch,
        ],
        compiler_params=pltpu.CompilerParams(vmem_limit_bytes=SCOPED + own),
        cost_estimate=pl.CostEstimate(
            flops=flops // COST, bytes_accessed=moved // COST, transcendentals=0
        ),
        name=name,
    )(flags, *inputs, *behind, *[pltpu.with_memory_space_constraint(w, pltpu.HBM) for w in weights])
    return result[:n_out], result[n_out:]


def load(flags, ahead, behind):
    def kernel(flag_ref, in_refs, out_refs, scratch_refs):
        out_refs[0][...] = jnp.full((8, 128), flag_ref[0], jnp.int32)

    (done,), pieces = call(
        kernel,
        "load",
        flags,
        [],
        [jax.ShapeDtypeStruct((8, 128), jnp.int32)],
        ahead,
        [],
        0,
        behind,
    )
    return done, pieces


def attend(lengths, queries, keys, values, new_keys, new_values, resid, gain):
    count, width = queries.shape
    cached = keys.shape[1]
    heads = width // HD
    groups = heads // KVH
    score_scale = 1.0 / HD**0.5
    inputs = (lengths, queries, keys, new_keys, values, new_values, resid)

    def kernel(*refs):
        slow_refs, gain_ref, refs = refs[: len(inputs)], refs[len(inputs)], refs[len(inputs) + 1 :]
        mixed_ref, square_ref, gain_out, *fast_refs, sems = refs
        length_ref, q_ref, k_ref, kn_ref, v_ref, vn_ref, resid_ref = fast_refs
        copies = [
            pltpu.make_async_copy(slow, fast, sems.at[i])
            for i, (slow, fast) in enumerate(zip(slow_refs, fast_refs, strict=True))
        ]
        copies.append(pltpu.make_async_copy(gain_ref, gain_out, sems.at[len(inputs)]))
        for copy in copies:
            copy.start()
        position = lax.broadcasted_iota(jnp.int32, (heads, cached), 1)
        owner = lax.broadcasted_iota(jnp.int32, (heads, HD), 0) // groups

        def rows_of(ref, b):
            row = ref[b : b + 1, :].astype(F32)
            return jnp.concatenate(
                [
                    jnp.broadcast_to(row[:, g * HD : (g + 1) * HD], (groups, HD))
                    for g in range(KVH)
                ],
                axis=0,
            )

        for copy in copies[:4]:
            copy.wait()
        weights = []
        for b in range(count):
            q = q_ref[b : b + 1, :].astype(F32).reshape(heads, HD)
            spread = jnp.concatenate(
                [jnp.where(owner == g, q, 0.0).astype(BF16) for g in range(KVH)], axis=1
            )
            scores = lax.dot_general(
                spread, k_ref[b], (((1,), (1,)), ((), ())), preferred_element_type=F32
            )
            scores = scores * score_scale
            own = jnp.sum(q * rows_of(kn_ref, b), axis=-1, keepdims=True) * score_scale
            live = position < length_ref[b]
            scores = jnp.where(live, scores, jnp.float32(-1e30))
            top = jnp.maximum(jnp.max(scores, axis=-1, keepdims=True), own)
            cache_exp = jnp.where(live, jnp.exp(scores - top), jnp.float32(0.0))
            own_exp = jnp.exp(own - top)
            total = jnp.sum(cache_exp, axis=-1, keepdims=True) + own_exp
            weights.append(
                ((cache_exp / total).astype(BF16), (own_exp / total).astype(BF16).astype(F32))
            )
        for copy in copies[4:]:
            copy.wait()
        for b in range(count):
            probs, own_prob = weights[b]
            product = jnp.dot(probs, v_ref[b], preferred_element_type=F32)
            attended = [
                product[g * groups : (g + 1) * groups, g * HD : (g + 1) * HD] for g in range(KVH)
            ]
            mixed = jnp.concatenate(attended, axis=0) + own_prob * rows_of(vn_ref, b)
            mixed = mixed + resid_ref[b : b + 1, :].astype(F32).reshape(heads, HD)
            mean_square = jnp.sum(mixed * mixed, keepdims=True) * (1.0 / width)
            mixed_ref[b : b + 1, :] = mixed.reshape(1, width)
            square_ref[b : b + 1, :] = jnp.broadcast_to(mean_square, (1, HD))

    fast = [pltpu.VMEM(x.shape, x.dtype) for x in inputs]
    fast[0] = pltpu.SMEM(lengths.shape, lengths.dtype)
    return pl.pallas_call(
        kernel,
        in_specs=[SLOW] * (len(inputs) + 1),
        out_specs=[FAST] * 3,
        out_shape=[
            jax.ShapeDtypeStruct((count, width), F32),
            jax.ShapeDtypeStruct((count, HD), F32),
            jax.ShapeDtypeStruct(gain.shape, gain.dtype),
        ],
        scratch_shapes=[*fast, pltpu.SemaphoreType.DMA((len(inputs) + 1,))],
        compiler_params=pltpu.CompilerParams(vmem_limit_bytes=16 << 20),
        name="attend",
    )(*[pltpu.with_memory_space_constraint(x, pltpu.HBM) for x in (*inputs, gain)])


def gate_up(core, x, gates, ups, ahead, behind, places=None, late=()):
    depth = gates[0].shape[0]
    pieces = [x] if places is None else x
    rows = x.shape[0] if places is None else sum(p.size for p in pieces) // depth
    half = rows // 2
    m = len(pieces)
    made = [] if places is None else [jax.ShapeDtypeStruct((rows, depth), BF16)]
    held, tile = len(gates), gates[0].shape[1]
    n = held + len(late) // 2

    def kernel(core_ref, in_refs, out_refs, scratch_refs, late_refs=(), copies=()):
        x_ref, w_refs = in_refs[0], (in_refs[m : held + m], in_refs[held + m :])
        *made_refs, keep_ref, send_ref = out_refs
        for x_ref in made_refs:
            for i in range(m):
                for source, count, row, column in places[i]:
                    x_ref[row : row + count, column : column + pieces[i].shape[1]] = in_refs[i][
                        source : source + count, :
                    ]
        upper = core_ref[0] == 0
        for j in range(n):
            at = slice(j * tile, (j + 1) * tile)
            for i in range(2):
                if j < held:
                    w_ref = w_refs[i][j]
                else:
                    w_ref = late_refs[2 * (j - held) + i]
                    copies[2 * (j - held) + i].wait()
                part = jnp.dot(x_ref[...], w_ref[...], preferred_element_type=F32)
                keep_ref[i, :, at] = jnp.where(upper, part[:half], part[half:])
                send_ref[i, :, at] = jnp.where(upper, part[half:], part[:half]).astype(BF16)

    return call(
        kernel,
        "gate_up",
        core,
        [*pieces, *gates, *ups],
        [
            *made,
            jax.ShapeDtypeStruct((2, half, n * tile), F32),
            jax.ShapeDtypeStruct((2, half, n * tile), BF16),
        ],
        ahead,
        [],
        4 * rows * depth * n * tile,
        behind,
        late,
    )


def down(core, mine, theirs, sums, weights, first, count, tile, split, ahead, behind):
    half = mine[0].shape[0]
    widths = [t.shape[1] for t in mine]
    n = len(mine)
    shapes = jax.eval_shape(split, jax.ShapeDtypeStruct((2 * half, tile), F32))
    with_sums = [] if sums is None else [sums]

    def kernel(core_ref, in_refs, out_refs, scratch_refs):
        (h_ref,) = scratch_refs
        own = pl.multiple_of(core_ref[0] * half, half)
        other = pl.multiple_of(half - core_ref[0] * half, half)
        at = 0
        for i in range(n):
            h_ref[pl.ds(own, half), at : at + widths[i]] = in_refs[i][...]
            h_ref[pl.ds(other, half), at : at + widths[i]] = in_refs[n + i][...]
            at += widths[i]
        for j in range(count):
            columns = slice((first + j) * tile, (first + j + 1) * tile)
            value, at = None, 0
            for i in range(n):
                term = jnp.dot(
                    h_ref[:, at : at + widths[i]],
                    in_refs[2 * n + i][:, columns],
                    preferred_element_type=F32,
                )
                value = term if value is None else value + term
                at += widths[i]
            for ref in in_refs[3 * n :]:
                value = value + ref[:, columns]
            for ref, part in zip(out_refs, split(value), strict=True):
                ref[:, j * tile : (j + 1) * tile] = part

    return call(
        kernel,
        "down",
        core,
        [*mine, *theirs, *weights, *with_sums],
        [jax.ShapeDtypeStruct((s.shape[0], count * tile), s.dtype) for s in shapes],
        ahead,
        [pltpu.VMEM((2 * half, sum(widths)), BF16)],
        4 * half * sum(widths) * count * tile,
        behind,
    )


def solution(mesh):
    n_wide, n_narrow = mesh.shape["wide"], mesh.shape["narrow"]
    n_far = n_wide // 2
    near_far = n_far // 2

    def narrow_swap(x, mask):
        return lax.ppermute(x, "narrow", [(i, i ^ mask) for i in range(n_narrow)])

    def wide_swap(x):
        return lax.ppermute(x, "wide", [(i, i ^ 1) for i in range(n_wide)])

    def far_swap(x, slot):
        return lax.ppermute(x, "wide", [(i, i ^ (slot << 1)) for i in range(n_wide)])

    def from_narrow(pieces, am, j):
        out = pieces[j]
        for i in range(1, n_narrow):
            out = jnp.where(am[i], pieces[j ^ i], out)
        return out

    def body(
        resid,
        queries,
        key_cache,
        value_cache,
        new_keys,
        new_values,
        lengths,
        norm_gain,
        w_gate,
        w_up,
        w_down,
    ):
        own_rows = resid.shape[0]
        block = w_gate.shape[0]
        me = lax.axis_index("narrow").astype(jnp.uint32)
        partner = [me ^ jnp.uint32(s) for s in range(n_narrow)]
        place = (
            [p * jnp.uint32(block) for p in partner],
            [p * jnp.uint32(own_rows) for p in partner],
            [me == jnp.uint32(i) for i in range(n_narrow)],
            (me & jnp.uint32(1)).astype(jnp.int32).reshape(1),
        )
        place, queries = lax.optimization_barrier((place, queries))
        column_at, row_at, am, core = place
        tile = tile_of(w_gate.shape[1])
        tiles = w_gate.shape[1] // tile
        middle = 1 + tiles // 2
        chunks = [[0], list(range(1, middle)), list(range(middle, tiles))]
        gates, ups, downs = {}, {}, {}

        def gate_up_pieces(which):
            return [
                Piece(w, 0, w.shape[0], j * tile, tile) for j in which for w in (w_gate, w_up)
            ]

        def take(which, pieces):
            for i, j in enumerate(which):
                gates[j], ups[j] = pieces[2 * i], pieces[2 * i + 1]

        def bring(which, behind):
            done, pieces = load(core, gate_up_pieces(which), behind)
            take(which, pieces)
            return done

        early = chunks[1] + chunks[2][:1]
        def down_pieces(which):
            return [
                Piece(w_down, chunks[c][0] * tile, len(chunks[c]) * tile, 0, w_down.shape[1])
                for c in which
            ]

        mixed, mean_square, gain = attend(
            lengths, queries, key_cache, value_cache, new_keys, new_values, resid, norm_gain
        )
        normed = (
            mixed * lax.rsqrt(mean_square[:, :1] + 1e-05) * gain.astype(F32)
        ).astype(BF16)
        def column_block(x, s):
            return lax.dynamic_slice(x, (jnp.uint32(0), column_at[s]), (own_rows, block))

        pieces = [column_block(normed, 0)]
        for s in range(1, n_narrow):
            pieces.append(narrow_swap(column_block(normed, s), s))
        done = bring(chunks[0], [normed])
        pieces, first_done = lax.optimization_barrier((pieces, done))
        group = jnp.concatenate([from_narrow(pieces, am, j) for j in range(n_narrow)], axis=0)
        group_rows = own_rows * n_narrow

        unit = tile_of(block)
        cut = (block // unit * 3 // 8) * unit
        left, right = group[:, :cut], group[:, cut:]
        pair = jnp.concatenate([left, wide_swap(left)], axis=0)
        far_right = [right] + [far_swap(right, s) for s in range(1, n_far)]
        done = bring(early[: len(early) // 2], [pair])
        pair, far_right, done = lax.optimization_barrier((pair, far_right, done))
        other = wide_swap(jnp.concatenate(far_right, axis=0))
        far_pairs = [pair] + [far_swap(pair, s) for s in range(1, n_far)]
        second_done = bring(early[len(early) // 2 :], [pair])
        far_pairs, other, second_done = lax.optimization_barrier((far_pairs, other, second_done))

        run = near_far * group_rows

        def row_of(far, near):
            return (2 * (far // near_far) + near) * run + far % near_far * group_rows

        x_pieces = [*far_pairs, *far_right, other]
        places = [
            *[
                [(side * group_rows, group_rows, row_of(s, side), 0) for side in range(2)]
                for s in range(n_far)
            ],
            *[[(0, group_rows, row_of(s, 0), cut)] for s in range(n_far)],
            [(s * group_rows, group_rows, row_of(s, 1), cut) for s in range(n_far)],
        ]

        plan = [[], [], down_pieces([0])]
        late = gate_up_pieces(chunks[2][1:])
        chips, arrived, mine, theirs = [], [], [], []

        def finish(c):
            total = chips[c]
            for part in arrived[c]:
                total = total + part.astype(F32)
            gate, up = total[0], total[1]
            if c == len(chunks) - 1:
                gate, up = chips[c][0], chips[c][1]
                for part in arrived[c]:
                    gate = gate + part[0].astype(F32)
                    up = up + part[1].astype(F32)
            hidden = (jax.nn.silu(gate) * up).astype(BF16)
            mine.append(hidden)

        for c, which in enumerate(chunks):
            behind = [sent] if c else [first_done, done, second_done]
            (*made, keep, send), pieces = gate_up(
                core,
                x if c else x_pieces,
                [gates[j] for j in which if j in gates],
                [ups[j] for j in which if j in ups],
                plan[c],
                behind,
                None if c else places,
                late if c == 2 else (),
            )
            if c == 0:
                (x,) = made
            elif c == 2:
                (downs[0],) = pieces
            chip = keep + narrow_swap(send, 1).astype(F32)
            sent = chip.astype(BF16)
            if c:
                finish(c - 1)
                sent, mine[c - 1] = lax.optimization_barrier((sent, mine[c - 1]))
            if c > 1:
                sent, theirs[0] = lax.optimization_barrier((sent, theirs[0]))
            if c:
                theirs.append(narrow_swap(mine[c - 1], 1))
            chips.append(chip)
            arrived.append([narrow_swap(sent, s) for s in range(2, n_narrow, 2)])

        column_tile = tile_of(w_down.shape[1])
        column_tiles = w_down.shape[1] // column_tile
        _, (downs[1],) = load(core, down_pieces([1]), [sent])
        (sums,), (downs[2],) = down(
            core,
            mine,
            theirs,
            None,
            [downs[0], downs[1]],
            0,
            column_tiles,
            column_tile,
            lambda value: (value,),
            down_pieces([2]),
            [],
        )
        sums, arrived[-1] = lax.optimization_barrier((sums, arrived[-1]))
        finish(len(chunks) - 1)
        theirs.append(narrow_swap(mine[-1], 1))

        near_tiles = column_tiles * 5 // 8
        def split_near(value):
            kept = [value[2 * top * run : (2 * top + 1) * run] for top in range(2)]
            sent = [value[(2 * top + 1) * run : (2 * top + 2) * run] for top in range(2)]
            return jnp.concatenate(kept, axis=0), jnp.concatenate(sent, axis=0).astype(BF16)

        def split_far(value):
            out = []
            for top in range(2):
                for low in range(near_far):
                    at = 2 * top * run + low * group_rows
                    both = [value[i : i + group_rows] for i in (at, at + run)]
                    out.append(jnp.concatenate(both, axis=0))
            return (out[0], *[part.astype(BF16) for part in out[1:]])

        (kept, sent), _ = down(
            core,
            mine[2:],
            theirs[2:],
            sums,
            [downs[2]],
            0,
            near_tiles,
            column_tile,
            split_near,
            [],
            [],
        )
        far_parts, _ = down(
            core,
            mine[2:],
            theirs[2:],
            sums,
            [downs[2]],
            near_tiles,
            column_tiles - near_tiles,
            column_tile,
            split_far,
            [],
            [sent],
        )
        near_sum = kept + wide_swap(sent).astype(F32)
        near_sent = near_sum.astype(BF16)
        left_sum = near_sum[:group_rows]
        right_parts = [far_swap(far_parts[s], s) for s in range(1, n_far)]
        left_parts = [
            far_swap(near_sent[s * group_rows : (s + 1) * group_rows], s) for s in range(1, n_far)
        ]
        right_parts, left_parts[0] = lax.optimization_barrier((right_parts, left_parts[0]))
        right_sum = far_parts[0]
        for part in right_parts:
            right_sum = right_sum + part.astype(F32)
        for part in left_parts:
            left_sum = left_sum + part.astype(F32)
        right_sum = right_sum[:group_rows] + wide_swap(
            right_sum[group_rows:].astype(BF16)
        ).astype(F32)
        reduced = jnp.concatenate([left_sum, right_sum], axis=1).astype(BF16)

        def row_block(x, s):
            return lax.dynamic_slice(x, (row_at[s], jnp.uint32(0)), (own_rows, block))

        pieces = [row_block(reduced, 0)]
        for s in range(1, n_narrow):
            pieces.append(narrow_swap(row_block(reduced, s), s))
        ffn_out = jnp.concatenate([from_narrow(pieces, am, j) for j in range(n_narrow)], axis=1)
        return (mixed + ffn_out.astype(F32)).astype(BF16)

    return jax.shard_map(
        body,
        mesh=mesh,
        in_specs=(
            P(("wide", "narrow"), None),
            P(("wide", "narrow"), None),
            P(("wide", "narrow"), None, None),
            P(("wide", "narrow"), None, None),
            P(("wide", "narrow"), None),
            P(("wide", "narrow"), None),
            P(("wide", "narrow")),
            P(),
            P("narrow", "wide"),
            P("narrow", "wide"),
            P("wide", "narrow"),
        ),
        out_specs=P(("wide", "narrow"), None),
        check_vma=False,
    )
```
